32 devices in a mesh: parts: 2 (over x), pool: 4 (over y, core), tp: 4 (over z).
Axes of the slice: x: 2, y: 2, z: 4, core: 2. Of those that a mesh axis runs over, the one named last changes fastest.
Arguments:
- residual: bfloat16 [512, 4096], P(('parts', 'pool', 'tp')), parts along dimension 0, may hold values from -6 to 6
- queries: bfloat16 [512, 2048], P(('parts', 'pool'), 'tp'), parts along dimension 0, may hold values from -24 to 24
- new_kv: bfloat16 [2, 512, 1024], P(None, ('parts', 'pool'), 'tp'), parts along dimension 1, may hold values from -4 to 4
- cache: bfloat16 [2, 16, 512, 1024], P(None, ('parts', 'pool'), None, 'tp'), parts along dimension 1, may hold values from -20 to 20
- cache_len: int32 [16], P(('parts', 'pool')), parts along dimension 0, may hold values from 128 to 512, as said below
- draft_count: int32 [16], P(('parts', 'pool')), parts along dimension 0, may hold values from 1 to 32, as said below
- out_proj: bfloat16 [2048, 4096], P('tp'), may hold values from -0.5 to 0.5
- norm_gain: float32 [4096], replicated, may hold values from 0.1 to 1.9
- routes: int32 [512, 2], P(('parts', 'pool', 'tp')), parts along dimension 0, may hold values from 0 to 3, as said below
- slots: int32 [512, 2], P(('parts', 'pool', 'tp')), parts along dimension 0, may hold values from -1 to 11, as said below
- route_weights: bfloat16 [512, 2], P(('parts', 'pool', 'tp')), parts along dimension 0, may hold values from 0.099609375 to 1
- w_gate: bfloat16 [4, 4096, 3200], P('pool', None, 'tp'), may hold values from -0.09375 to 0.09375
- w_up: bfloat16 [4, 4096, 3200], P('pool', None, 'tp'), may hold values from -0.09375 to 0.09375
- w_down: bfloat16 [4, 3200, 4096], P('pool', 'tp'), may hold values from -0.109375 to 0.109375
Outputs:
- mixed: bfloat16 [512, 4096], P(('parts', 'pool', 'tp')), parts along dimension 0
The draws below stay inside these ranges and needn't reach their ends.
There are 2 independent parts, one for each index of `parts`. The reference program is written for one: setup_inputs(seed, part) draws one part's arguments, and reference() takes and returns one part's arrays. A program takes and returns all parts, laid end to end along the dimension named above; an argument that names none is the same for every part. Nothing has to cross between parts.
Inputs may be any that keep to these rules, and one draw needn't show every extreme that they name: `cache_len`: some request has a full cache. `draft_count`: some request has 32 draft rows. `routes`: the 2 ids of a row differ. Within the rows of one device, the routes to one expert taken in order of row and then of k get slots 0, 1, 2 and so on; those past the first 12 get -1; in every draw some expert gets all 12 slots from every device.
All inputs are finite; a program needn't handle non-finite values.
Results may differ from the reference program's by a relative error of at most 0.015.
Values may be sent and summed in bfloat16 or wider, within the bound.
A program may use at most 64 MiB of HBM per device.

```python
import jax
import jax.numpy as jnp
from jax import lax

D = 4096
HEADS = 16
KV = 8
HD = 128
FF = 3200
TOP = 2
DRAFT = 32
CACHE = 512
EXPERTS = 4
REQS = 8
ROWS = 256
ROW_DEV = 16
CAP = 12
N_TP = 4


def attention_draw(key):
    key_query, key_new, key_cache = jax.random.split(jax.random.fold_in(key, 11), 3)
    query_all = jnp.clip(jax.random.normal(key_query, (REQS, DRAFT, KV, HEADS // KV, HD), jnp.float32), -4.0, 4.0)
    new_all = jnp.clip(jax.random.normal(key_new, (2, REQS * DRAFT, KV * HD), jnp.float32), -4.0, 4.0)
    cache_all = jnp.clip(jax.random.normal(key_cache, (2, REQS, CACHE, KV, HD), jnp.float32), -4.0, 4.0)
    return (query_all.reshape(REQS * DRAFT, HEADS * HD), new_all, cache_all.reshape(2, REQS, CACHE, KV * HD))


def draw_queries(key, part):
    return attention_draw(key)[0].astype(jnp.bfloat16)


def draw_new_kv(key, part):
    return attention_draw(key)[1].astype(jnp.bfloat16)


def draw_cache(key, part):
    return attention_draw(key)[2].astype(jnp.bfloat16)


def draw_cache_len(key, part):
    key_first, key_second = jax.random.split(jax.random.fold_in(key, 23))
    lengths = jax.random.randint(key_first, (REQS,), CACHE // 4, CACHE + 1)
    chosen = jax.random.randint(key_second, (), 0, REQS)
    return jnp.where(jnp.arange(REQS) == chosen, CACHE, lengths).astype(jnp.int32)


def draw_draft_count(key, part):
    key_first, key_second = jax.random.split(jax.random.fold_in(key, 29))
    counts = jax.random.randint(key_first, (REQS,), 1, DRAFT + 1)
    chosen = jax.random.randint(key_second, (), 0, REQS)
    return jnp.where(jnp.arange(REQS) == chosen, DRAFT, counts).astype(jnp.int32)


def route_draw(key):
    key_hot, key_first, key_offset, key_score, key_side = jax.random.split(jax.random.fold_in(key, 31), 5)
    block_count = ROWS // ROW_DEV
    hot_expert = jax.random.randint(key_hot, (), 0, EXPERTS)
    first_pick = jax.random.randint(key_first, (block_count, ROW_DEV), 0, EXPERTS)
    offset = jax.random.randint(key_offset, (block_count, ROW_DEV), 1, EXPERTS)
    second = (first_pick + offset) % EXPERTS
    scores = jax.random.randint(key_score, (block_count, ROW_DEV), 0, 1 << 20) * ROW_DEV + jnp.arange(ROW_DEV)[None, :]
    unused, chosen = lax.top_k(scores, CAP)
    forced = jnp.any(chosen[:, :, None] == jnp.arange(ROW_DEV)[None, None, :], axis=1)
    side_pick = jax.random.randint(key_side, (block_count, ROW_DEV), 0, 2)
    partner = (hot_expert + offset) % EXPERTS
    pick_one = jnp.where(forced, jnp.where(side_pick == 0, hot_expert, partner), first_pick)
    pick_two = jnp.where(forced, jnp.where(side_pick == 0, partner, hot_expert), second)
    route_ids = jnp.stack([pick_one, pick_two], axis=-1).astype(jnp.int32)
    flat_ids = route_ids.reshape(block_count, ROW_DEV * TOP)
    one_hot = (flat_ids[:, :, None] == jnp.arange(EXPERTS)[None, None, :]).astype(jnp.int32)
    running = jnp.cumsum(one_hot, axis=1)
    rank_in = jnp.sum(running * one_hot, axis=-1) - 1
    slot_ids = jnp.where(rank_in < CAP, rank_in, -1)
    return (route_ids.reshape(ROWS, TOP), slot_ids.reshape(ROWS, TOP).astype(jnp.int32))


def draw_routes(key, part):
    return route_draw(key)[0]


def draw_slots(key, part):
    return route_draw(key)[1]


def block_scale(key, dims, pieces, least, high):
    def one(dim, parts):
        steps = jax.random.uniform(jax.random.fold_in(jax.random.fold_in(key, 6), dim), (parts,), jnp.float32, least / len(pieces), high / len(pieces))
        return jnp.repeat(jnp.exp(steps), dims[dim] // parts).reshape((-1,) + (1,) * (len(dims) - dim - 1))

    factor_of = one(*pieces[0])
    for cut in pieces[1:]:
        factor_of = factor_of * one(*cut)
    return factor_of


def bell_draw(stream_key, shape, spread, most, shards=(), dtype=jnp.bfloat16):
    drawn = jax.random.normal(stream_key, shape, jnp.float32) * spread
    if len(shards) > 0:
        drawn = block_scale(stream_key, shape, shards, -0.22, 0.18) * drawn
    return jnp.clip(drawn, min=-most, max=most).astype(dtype)


def setup_inputs(seed: int = 0, part: int = 0) -> dict:
    streams_of = jax.random.split(jax.random.key(seed), 15)
    own_keys = jax.random.split(jax.random.fold_in(streams_of[14], part), 15)
    return {
        "residual": bell_draw(own_keys[0], (ROWS, D), 1.0, 6.0, ((0, 16),)),
        "queries": draw_queries(jax.random.fold_in(jax.random.fold_in(streams_of[14], part), 71), part),
        "new_kv": draw_new_kv(jax.random.fold_in(jax.random.fold_in(streams_of[14], part), 71), part),
        "cache": draw_cache(jax.random.fold_in(jax.random.fold_in(streams_of[14], part), 71), part),
        "cache_len": draw_cache_len(jax.random.fold_in(jax.random.fold_in(streams_of[14], part), 71), part),
        "draft_count": draw_draft_count(jax.random.fold_in(jax.random.fold_in(streams_of[14], part), 71), part),
        "out_proj": bell_draw(streams_of[6], (HEADS * HD, D), HD ** -0.5, 0.5, ((0, 4),)),
        "norm_gain": jnp.clip(1.0 + 0.18 * jax.random.normal(streams_of[7], (D,), jnp.float32), 0.1, 1.9),
        "routes": draw_routes(jax.random.fold_in(jax.random.fold_in(streams_of[14], part), 71), part),
        "slots": draw_slots(jax.random.fold_in(jax.random.fold_in(streams_of[14], part), 71), part),
        "route_weights": jnp.clip(0.099609375 + 0.9003906 * jax.random.uniform(own_keys[10], (ROWS, TOP), jnp.float32) ** block_scale(own_keys[10], (ROWS, TOP), ((0, 16),), -0.2, 0.2), 0.099609375, 1.0).astype(jnp.bfloat16),
        "w_gate": bell_draw(streams_of[11], (EXPERTS, D, FF), D ** -0.5, 0.09375, ((0, 4), (2, 4))),
        "w_up": bell_draw(streams_of[12], (EXPERTS, D, FF), D ** -0.5, 0.09375, ((0, 4), (2, 4))),
        "w_down": bell_draw(streams_of[13], (EXPERTS, FF, D), FF ** -0.5, 0.109375, ((0, 4), (1, 4))),
    }


def reference(residual, queries, new_kv, cache, cache_len, draft_count, out_proj, norm_gain, routes, slots, route_weights, w_gate, w_up, w_down):
    group_size = HEADS // KV
    score_scale = HD ** (-0.5)

    def one_request(bundle):
        query_rows, key_new, value_new, key_old, value_old, length, live_count = bundle
        query_four = query_rows.reshape(DRAFT, KV, group_size, HD).astype(jnp.float32)
        key_new = key_new.reshape(DRAFT, KV, HD).astype(jnp.float32)
        value_new = value_new.reshape(DRAFT, KV, HD).astype(jnp.float32)
        key_old = key_old.reshape(CACHE, KV, HD).astype(jnp.float32)
        value_old = value_old.reshape(CACHE, KV, HD).astype(jnp.float32)
        score_old = jnp.einsum('jkgd,pkd->kgjp', query_four, key_old) * score_scale
        score_new = jnp.einsum('jkgd,ikd->kgji', query_four, key_new) * score_scale
        see_old = jnp.arange(CACHE) < length
        draft_index = jnp.arange(DRAFT)
        see_new = (draft_index[None, :] <= draft_index[:, None]) & (draft_index[None, :] < live_count)
        row_max = jnp.maximum(lax.optimization_barrier(jnp.max(jnp.where(see_old, score_old, -1e+30), axis=-1)), lax.optimization_barrier(jnp.max(jnp.where(see_new, score_new, -1e+30), axis=-1)))
        prob_old = jnp.where(see_old, jnp.exp(score_old - row_max[..., None]), 0.0)
        prob_new = jnp.where(see_new, jnp.exp(score_new - row_max[..., None]), 0.0)
        totals = lax.optimization_barrier(jnp.sum(prob_old, axis=-1)) + lax.optimization_barrier(jnp.sum(prob_new, axis=-1))
        weight_old = lax.optimization_barrier((prob_old / totals[..., None]).astype(jnp.bfloat16)).astype(jnp.float32)
        weight_new = lax.optimization_barrier((prob_new / totals[..., None]).astype(jnp.bfloat16)).astype(jnp.float32)
        output = jnp.einsum('kgjp,pkd->jkgd', weight_old, value_old) + jnp.einsum('kgji,ikd->jkgd', weight_new, value_new)
        return output.reshape(DRAFT, HEADS * HD).astype(jnp.bfloat16)
    attended = lax.map(one_request, (queries.reshape(REQS, DRAFT, HEADS * HD), new_kv[0].reshape(REQS, DRAFT, KV * HD), new_kv[1].reshape(REQS, DRAFT, KV * HD), cache[0], cache[1], cache_len, draft_count)).reshape(ROWS, HEADS * HD)
    projected = jnp.dot(attended, out_proj, preferred_element_type=jnp.float32)
    hidden_state = (residual.astype(jnp.float32) + projected).astype(jnp.bfloat16)
    hidden_wide = hidden_state.astype(jnp.float32)
    power = lax.optimization_barrier(jnp.mean(hidden_wide * hidden_wide, axis=1, keepdims=True))
    normed = (hidden_wide * lax.rsqrt(power + 1e-05) * norm_gain.astype(jnp.float32)).astype(jnp.bfloat16)
    block_count = ROWS // ROW_DEV
    block_of = (jnp.arange(ROWS) // ROW_DEV).astype(jnp.int32)
    is_valid = slots >= 0
    spare = block_count * EXPERTS * CAP
    target = block_of[:, None] * (EXPERTS * CAP) + routes * CAP + slots
    target = jnp.where(is_valid, target, spare).astype(jnp.int32)
    dispatched = jnp.zeros((spare + 1, D), jnp.bfloat16).at[target.reshape(-1)].set(jnp.repeat(normed, TOP, axis=0))
    per_expert = dispatched[:spare].reshape(block_count, EXPERTS, CAP, D).transpose(1, 0, 2, 3).reshape(EXPERTS, block_count * CAP, D)
    slice_width = FF // N_TP

    def serve_rows(bundle):
        row_block, gate_w, up_w, down_w = bundle
        gate_val = jnp.dot(row_block, gate_w, preferred_element_type=jnp.float32)
        up_val = jnp.dot(row_block, up_w, preferred_element_type=jnp.float32)
        activated = (jax.nn.silu(gate_val) * up_val).astype(jnp.bfloat16)
        totals = jnp.zeros((row_block.shape[0], D), jnp.float32)
        for part_index in range(N_TP):
            low_col = part_index * slice_width
            partial_sum = jnp.dot(activated[:, low_col:low_col + slice_width], down_w[low_col:low_col + slice_width], preferred_element_type=jnp.float32)
            totals = totals + lax.optimization_barrier(partial_sum.astype(jnp.bfloat16)).astype(jnp.float32)
        return totals.astype(jnp.bfloat16)
    served = lax.map(serve_rows, (per_expert, w_gate, w_up, w_down))
    flat_out = served.reshape(EXPERTS, block_count, CAP, D).transpose(1, 0, 2, 3).reshape(spare, D)
    flat_out = jnp.concatenate([flat_out, jnp.zeros((1, D), jnp.bfloat16)], axis=0)
    picked = flat_out[target]
    combine_w = jnp.where(is_valid, route_weights.astype(jnp.float32), 0.0)
    moe_sum = lax.optimization_barrier(jnp.sum(picked.astype(jnp.float32) * combine_w[:, :, None], axis=1))
    return (hidden_wide + moe_sum).astype(jnp.bfloat16)
```

```python
import functools

import jax
import jax.numpy as jnp
from jax import lax
from jax.experimental import pallas as pl
from jax.experimental.pallas import tpu as pltpu
from jax.sharding import PartitionSpec as P

HD = 128
LANES = 128
CORES = 2
MESH = pl.DeviceIdType.MESH
F32 = jnp.float32
BF16 = jnp.bfloat16


def remote(src, dst, send_sem, recv_sem, where):
    return pltpu.make_async_remote_copy(
        src_ref=src,
        dst_ref=dst,
        send_sem=send_sem,
        recv_sem=recv_sem,
        device_id=where,
        device_id_type=MESH,
    )


def kernel(
    pool_count,
    tp_count,
    chunks,
    cache_len,
    draft_count,
    routes,
    slots,
    route_weights,
    residual_hbm,
    queries_hbm,
    new_kv_hbm,
    cache_hbm,
    out_proj_hbm,
    gain_hbm,
    w_gate_hbm,
    w_up_hbm,
    w_down_hbm,
    out_ref,
    residual,
    queries,
    new_kv,
    cache,
    out_proj,
    gain,
    w_gate,
    w_up,
    w_down,
    attended,
    proj_part,
    proj_in,
    hidden,
    rows_all,
    weights_all,
    gate_acc,
    up_acc,
    act,
    part_all,
    core_in,
    pair_in,
    pair_sum,
    line_in,
    load_sem,
    ps_sem,
    pr_sem,
    wzs_sem,
    wzr_sem,
    wys_sem,
    wyr_sem,
    wc_sem,
    gzs_sem,
    gzr_sem,
    gys_sem,
    gyr_sem,
    gcs_sem,
    gcr_sem,
    szs_sem,
    szr_sem,
    sys_sem,
    syr_sem,
    scs_sem,
    scr_sem,
):
    y_count = pool_count // CORES
    pool_me = lax.axis_index("pool")
    z_me = lax.axis_index("tp")
    y_me = pool_me // CORES
    c_me = lax.rem(pool_me, CORES)
    c_other = 1 - c_me
    core_dev = {"pool": y_me * CORES + c_other}

    def z_at(step):
        return lax.rem(z_me + step, tp_count)

    def y_at(step):
        return lax.rem(y_me + step, y_count)

    def z_dev(z):
        return {"tp": z}

    def y_dev(y):
        return {"pool": y * CORES + c_me}

    rows, dim = residual.shape
    line_rows = tp_count * rows
    half_rows = y_count * line_rows
    all_rows = CORES * half_rows
    width = dim // chunks

    def cols(k):
        return pl.ds(pl.multiple_of(k * width, width), width)

    def row_ds(start, size):
        return pl.ds(pl.multiple_of(start, size), size)

    loads = [
        pltpu.make_async_copy(src, dst, load_sem.at[n])
        for n, (src, dst) in enumerate(
            [
                (queries_hbm, queries),
                (cache_hbm, cache),
                (new_kv_hbm, new_kv),
                (out_proj_hbm, out_proj),
                (residual_hbm, residual),
                (gain_hbm, gain),
                (w_gate_hbm, w_gate),
                (w_up_hbm, w_up),
                (w_down_hbm, w_down),
            ]
        )
    ]
    for load in loads:
        load.start()

    barrier = pltpu.get_barrier_semaphore()
    partners = (
        [core_dev]
        + [y_dev(y_at(s)) for s in range(1, y_count)]
        + [z_dev(z_at(s)) for s in range(1, tp_count)]
    )
    for partner in partners:
        pl.semaphore_signal(barrier, inc=1, device_id=partner, device_id_type=MESH)
    pl.semaphore_wait(barrier, len(partners))

    half_at = c_me * half_rows
    line_at = half_at + y_me * line_rows
    own_at = line_at + z_me * rows

    lane = lax.broadcasted_iota(jnp.int32, (rows, weights_all.shape[1]), 1)
    dense = jnp.zeros((rows, weights_all.shape[1]), F32)
    for k in range(routes.shape[1]):
        hit = (routes[:, k : k + 1] == lane) & (slots[:, k : k + 1] >= 0)
        dense = dense + jnp.where(hit, route_weights[:, k : k + 1].astype(F32), 0.0)
    weights_all[row_ds(own_at, rows), :] = dense.astype(BF16)

    def w_line(step, z_from):
        block = weights_all.at[row_ds(line_at + z_from * rows, rows), :]
        z_to = z_at(step)
        return block, z_to

    def w_z_send(step):
        block = weights_all.at[row_ds(own_at, rows), :]
        z_to = z_at(step)
        return remote(block, block, wzs_sem.at[z_to], wzr_sem.at[z_me], z_dev(z_to))

    def w_z_recv(step):
        z_from = z_at(step)
        block = weights_all.at[row_ds(line_at + z_from * rows, rows), :]
        return remote(block, block, wzs_sem.at[z_from], wzr_sem.at[z_from], z_dev(z_from))

    def w_y_send(step):
        block = weights_all.at[row_ds(line_at, line_rows), :]
        y_to = y_at(step)
        return remote(block, block, wys_sem.at[y_to], wyr_sem.at[y_me], y_dev(y_to))

    def w_y_recv(step):
        y_from = y_at(step)
        block = weights_all.at[row_ds(half_at + y_from * line_rows, line_rows), :]
        return remote(block, block, wys_sem.at[y_from], wyr_sem.at[y_from], y_dev(y_from))

    def w_c_send():
        block = weights_all.at[row_ds(half_at, half_rows), :]
        return remote(block, block, wc_sem.at[0], wc_sem.at[1], core_dev)

    def w_c_recv():
        block = weights_all.at[row_ds(c_other * half_rows, half_rows), :]
        return remote(block, block, wc_sem.at[0], wc_sem.at[1], core_dev)

    for s in range(1, tp_count):
        w_z_send(s).start()

    for load in loads[:3]:
        load.wait()
    requests, cache_size = cache.shape[1], cache.shape[2]
    kv_here = cache.shape[3] // HD
    draft = queries.shape[0] // requests
    group = queries.shape[1] // HD // kv_here
    scale = HD ** (-0.5)
    nt = (((1,), (1,)), ((), ()))
    for r in range(requests):
        span = slice(r * draft, (r + 1) * draft)
        for h in range(kv_here):
            kv_cols = slice(h * HD, (h + 1) * HD)
            q = jnp.concatenate(
                [
                    queries[span, (h * group + g) * HD : (h * group + g + 1) * HD]
                    for g in range(group)
                ],
                axis=0,
            )
            old = lax.dot_general(q, cache[0, r, :, kv_cols], nt, preferred_element_type=F32) * scale
            new = lax.dot_general(q, new_kv[0, span, kv_cols], nt, preferred_element_type=F32) * scale
            old_at = lax.broadcasted_iota(jnp.int32, old.shape, 1)
            new_at = lax.broadcasted_iota(jnp.int32, new.shape, 1)
            new_row = lax.rem(lax.broadcasted_iota(jnp.int32, new.shape, 0), draft)
            see_old = old_at < cache_len[r]
            see_new = (new_at <= new_row) & (new_at < draft_count[r])
            top = jnp.maximum(
                jnp.max(jnp.where(see_old, old, -1e30), axis=1, keepdims=True),
                jnp.max(jnp.where(see_new, new, -1e30), axis=1, keepdims=True),
            )
            p_old = jnp.where(see_old, jnp.exp(old - top), 0.0)
            p_new = jnp.where(see_new, jnp.exp(new - top), 0.0)
            total = jnp.sum(p_old, axis=1, keepdims=True) + jnp.sum(p_new, axis=1, keepdims=True)
            a_old = (p_old / total).astype(BF16)
            a_new = (p_new / total).astype(BF16)
            res = jnp.dot(a_old, cache[1, r, :, kv_cols], preferred_element_type=F32)
            res = res + jnp.dot(a_new, new_kv[1, span, kv_cols], preferred_element_type=F32)
            for g in range(group):
                attended[span, (h * group + g) * HD : (h * group + g + 1) * HD] = res[
                    g * draft : (g + 1) * draft
                ].astype(BF16)

    def proj_send(k, step):
        z_to = z_at(step)
        return remote(
            proj_part.at[row_ds(z_to * rows, rows), cols(k)],
            proj_in.at[z_me, :, cols(k)],
            ps_sem.at[k, z_to],
            pr_sem.at[k, z_me],
            z_dev(z_to),
        )

    def proj_recv(k, step):
        z_from = z_at(step)
        block = proj_in.at[z_from, :, cols(k)]
        return remote(
            proj_part.at[row_ds(z_from * rows, rows), cols(k)],
            block,
            ps_sem.at[k, z_from],
            pr_sem.at[k, z_from],
            z_dev(z_from),
        )

    loads[3].wait()

    def project(k, carry):
        proj_part[:, cols(k)] = jnp.dot(
            attended[...], out_proj[:, cols(k)], preferred_element_type=F32
        ).astype(BF16)
        for s in range(1, tp_count):
            proj_send(k, s).start()
        return carry

    lax.fori_loop(0, chunks, project, 0)

    for s in range(1, tp_count):
        w_z_recv(s).wait_recv()
    for s in range(1, y_count):
        w_y_send(s).start()
    for s in range(1, y_count):
        w_y_recv(s).wait_recv()
    w_c_send().start()

    loads[4].wait()
    loads[5].wait()

    def add_residual(k, power):
        for s in range(1, tp_count):
            proj_recv(k, s).wait_recv()
        total = proj_part[row_ds(z_me * rows, rows), cols(k)].astype(F32)
        for s in range(1, tp_count):
            total = total + proj_in[z_at(s), :, cols(k)].astype(F32)
        h = (residual[:, cols(k)].astype(F32) + total).astype(BF16)
        hidden[:, cols(k)] = h
        wide = h.astype(F32)
        return power + jnp.sum(wide * wide, axis=1, keepdims=True)

    power = lax.fori_loop(0, chunks, add_residual, jnp.zeros((rows, 1), F32))
    factor = lax.rsqrt(power / dim + 1e-05)

    def g_z_send(k, step):
        z_to = z_at(step)
        block = rows_all.at[row_ds(own_at, rows), cols(k)]
        return remote(block, block, gzs_sem.at[k, z_to], gzr_sem.at[k, z_me], z_dev(z_to))

    def g_z_recv(k, step):
        z_from = z_at(step)
        block = rows_all.at[row_ds(line_at + z_from * rows, rows), cols(k)]
        return remote(block, block, gzs_sem.at[k, z_from], gzr_sem.at[k, z_from], z_dev(z_from))

    def g_y_send(k, step):
        y_to = y_at(step)
        block = rows_all.at[row_ds(line_at, line_rows), cols(k)]
        return remote(block, block, gys_sem.at[k, y_to], gyr_sem.at[k, y_me], y_dev(y_to))

    def g_y_recv(k, step):
        y_from = y_at(step)
        block = rows_all.at[row_ds(half_at + y_from * line_rows, line_rows), cols(k)]
        return remote(block, block, gys_sem.at[k, y_from], gyr_sem.at[k, y_from], y_dev(y_from))

    def g_c_send(k):
        block = rows_all.at[row_ds(half_at, half_rows), cols(k)]
        return remote(block, block, gcs_sem.at[k], gcr_sem.at[k], core_dev)

    def g_c_recv(k):
        block = rows_all.at[row_ds(c_other * half_rows, half_rows), cols(k)]
        return remote(block, block, gcs_sem.at[k], gcr_sem.at[k], core_dev)

    def norm(k, carry):
        normed = hidden[:, cols(k)].astype(F32) * factor * gain[:, cols(k)]
        rows_all[row_ds(own_at, rows), cols(k)] = normed.astype(BF16)
        for s in range(1, tp_count):
            g_z_send(k, s).start()
        return carry

    lax.fori_loop(0, chunks, norm, 0)

    gate_acc[...] = jnp.zeros_like(gate_acc)
    up_acc[...] = jnp.zeros_like(up_acc)
    w_c_recv().wait_recv()
    loads[6].wait()
    loads[7].wait()

    def first(i, carry):
        @pl.when(i < chunks)
        def _():
            for s in range(1, tp_count):
                g_z_recv(i, s).wait_recv()
            for s in range(1, y_count):
                g_y_send(i, s).start()

        @pl.when((i >= 1) & (i < chunks + 1))
        def _():
            for s in range(1, y_count):
                g_y_recv(i - 1, s).wait_recv()
            g_c_send(i - 1).start()

        @pl.when(i >= 2)
        def _():
            k = i - 2
            g_c_recv(k).wait_recv()
            block = rows_all[:, cols(k)]
            gate_acc[...] += jnp.dot(block, w_gate[0, cols(k), :], preferred_element_type=F32)
            up_acc[...] += jnp.dot(block, w_up[0, cols(k), :], preferred_element_type=F32)

        return carry

    lax.fori_loop(0, chunks + 2, first, 0)

    gate = gate_acc[...]
    act[...] = (gate / (1.0 + jnp.exp(-gate)) * up_acc[...]).astype(BF16)
    expert_lane = lax.broadcasted_iota(jnp.int32, weights_all.shape, 1) == pool_me
    combine = jnp.sum(
        jnp.where(expert_lane, weights_all[...].astype(F32), 0.0), axis=1, keepdims=True
    )

    def s_c_send(k):
        return remote(
            part_all.at[row_ds(c_other * half_rows, half_rows), cols(k)],
            core_in.at[:, cols(k)],
            scs_sem.at[k],
            scr_sem.at[k],
            core_dev,
        )

    def s_y_send(k, step):
        y_to = y_at(step)
        return remote(
            core_in.at[row_ds(y_to * line_rows, line_rows), cols(k)],
            pair_in.at[y_me, :, cols(k)],
            sys_sem.at[k, y_to],
            syr_sem.at[k, y_me],
            y_dev(y_to),
        )

    def s_y_recv(k, step):
        y_from = y_at(step)
        return remote(
            core_in.at[row_ds(y_from * line_rows, line_rows), cols(k)],
            pair_in.at[y_from, :, cols(k)],
            sys_sem.at[k, y_from],
            syr_sem.at[k, y_from],
            y_dev(y_from),
        )

    def s_z_send(k, step):
        z_to = z_at(step)
        return remote(
            pair_sum.at[row_ds(z_to * rows, rows), cols(k)],
            line_in.at[z_me, :, cols(k)],
            szs_sem.at[k, z_to],
            szr_sem.at[k, z_me],
            z_dev(z_to),
        )

    def s_z_recv(k, step):
        z_from = z_at(step)
        return remote(
            pair_sum.at[row_ds(z_from * rows, rows), cols(k)],
            line_in.at[z_from, :, cols(k)],
            szs_sem.at[k, z_from],
            szr_sem.at[k, z_from],
            z_dev(z_from),
        )

    loads[8].wait()

    def second(i, carry):
        @pl.when(i < chunks)
        def _():
            part = jnp.dot(act[...], w_down[0, :, cols(i)], preferred_element_type=F32)
            part_all[:, cols(i)] = (part * combine).astype(BF16)
            s_c_send(i).start()

        @pl.when((i >= 1) & (i < chunks + 1))
        def _():
            k = i - 1
            s_c_send(k).wait_recv()
            core_in[:, cols(k)] = (
                core_in[:, cols(k)].astype(F32)
                + part_all[row_ds(half_at, half_rows), cols(k)].astype(F32)
            ).astype(BF16)
            for s in range(1, y_count):
                s_y_send(k, s).start()

        @pl.when((i >= 2) & (i < chunks + 2))
        def _():
            k = i - 2
            total = core_in[row_ds(y_me * line_rows, line_rows), cols(k)].astype(F32)
            for s in range(1, y_count):
                s_y_recv(k, s).wait_recv()
                total = total + pair_in[y_at(s), :, cols(k)].astype(F32)
            pair_sum[:, cols(k)] = total.astype(BF16)
            for s in range(1, tp_count):
                s_z_send(k, s).start()

        @pl.when(i >= 3)
        def _():
            k = i - 3
            total = pair_sum[row_ds(z_me * rows, rows), cols(k)].astype(F32)
            for s in range(1, tp_count):
                s_z_recv(k, s).wait_recv()
                total = total + line_in[z_at(s), :, cols(k)].astype(F32)
            out_ref[:, cols(k)] = (hidden[:, cols(k)].astype(F32) + total).astype(BF16)

        return carry

    lax.fori_loop(0, chunks + 3, second, 0)

    for s in range(1, tp_count):
        w_z_send(s).wait_send()
    for s in range(1, y_count):
        w_y_send(s).wait_send()
    w_c_send().wait_send()

    def drain(k, carry):
        for s in range(1, tp_count):
            proj_send(k, s).wait_send()
            g_z_send(k, s).wait_send()
            s_z_send(k, s).wait_send()
        for s in range(1, y_count):
            g_y_send(k, s).wait_send()
            s_y_send(k, s).wait_send()
        g_c_send(k).wait_send()
        s_c_send(k).wait_send()
        return carry

    lax.fori_loop(0, chunks, drain, 0)


def local(
    pool_count,
    tp_count,
    residual,
    queries,
    new_kv,
    cache,
    cache_len,
    draft_count,
    out_proj,
    norm_gain,
    routes,
    slots,
    route_weights,
    w_gate,
    w_up,
    w_down,
):
    rows, dim = residual.shape
    y_count = pool_count // CORES
    line_rows = tp_count * rows
    half_rows = y_count * line_rows
    all_rows = CORES * half_rows
    hidden_units = w_gate.shape[2]
    weight_lanes = pl.cdiv(pool_count, LANES) * LANES
    chunks = 4
    gain = norm_gain.reshape(1, dim)
    dma = pltpu.SemaphoreType.DMA
    loaded = (residual, queries, new_kv, cache, out_proj, gain, w_gate, w_up, w_down)
    smem = pl.BlockSpec(memory_space=pltpu.SMEM)
    vmem = pl.BlockSpec(memory_space=pltpu.VMEM)
    return pl.pallas_call(
        functools.partial(kernel, pool_count, tp_count, chunks),
        out_shape=jax.ShapeDtypeStruct((rows, dim), BF16),
        in_specs=[smem] * 2 + [vmem] * 3 + [pl.BlockSpec(memory_space=pl.ANY)] * len(loaded),
        out_specs=vmem,
        scratch_shapes=[pltpu.VMEM(a.shape, a.dtype) for a in loaded]
        + [
            pltpu.VMEM((queries.shape[0], queries.shape[1]), BF16),
            pltpu.VMEM((line_rows, dim), BF16),
            pltpu.VMEM((tp_count, rows, dim), BF16),
            pltpu.VMEM((rows, dim), BF16),
            pltpu.VMEM((all_rows, dim), BF16),
            pltpu.VMEM((all_rows, weight_lanes), BF16),
            pltpu.VMEM((all_rows, hidden_units), F32),
            pltpu.VMEM((all_rows, hidden_units), F32),
            pltpu.VMEM((all_rows, hidden_units), BF16),
            pltpu.VMEM((all_rows, dim), BF16),
            pltpu.VMEM((half_rows, dim), BF16),
            pltpu.VMEM((y_count, line_rows, dim), BF16),
            pltpu.VMEM((line_rows, dim), BF16),
            pltpu.VMEM((tp_count, rows, dim), BF16),
            dma((len(loaded),)),
            dma((chunks, tp_count)),
            dma((chunks, tp_count)),
            dma((tp_count,)),
            dma((tp_count,)),
            dma((y_count,)),
            dma((y_count,)),
            dma((2,)),
            dma((chunks, tp_count)),
            dma((chunks, tp_count)),
            dma((chunks, y_count)),
            dma((chunks, y_count)),
            dma((chunks,)),
            dma((chunks,)),
            dma((chunks, tp_count)),
            dma((chunks, tp_count)),
            dma((chunks, y_count)),
            dma((chunks, y_count)),
            dma((chunks,)),
            dma((chunks,)),
        ],
        compiler_params=pltpu.CompilerParams(
            collective_id=0, has_side_effects=True, vmem_limit_bytes=60 * 1024 * 1024
        ),
    )(cache_len, draft_count, routes, slots, route_weights, *loaded)


def solution(mesh):
    in_specs = (
        P(("parts", "pool", "tp"), None),
        P(("parts", "pool"), "tp"),
        P(None, ("parts", "pool"), "tp"),
        P(None, ("parts", "pool"), None, "tp"),
        P(("parts", "pool")),
        P(("parts", "pool")),
        P("tp", None),
        P(),
        P(("parts", "pool", "tp"), None),
        P(("parts", "pool", "tp"), None),
        P(("parts", "pool", "tp"), None),
        P("pool", None, "tp"),
        P("pool", None, "tp"),
        P("pool", "tp", None),
    )
    out_specs = P(("parts", "pool", "tp"), None)
    body = functools.partial(local, mesh.shape["pool"], mesh.shape["tp"])
    return jax.shard_map(body, mesh=mesh, in_specs=in_specs, out_specs=out_specs, check_vma=False)
```

```python
import functools

import jax
import jax.numpy as jnp
from jax import lax
from jax.experimental import pallas as pl
from jax.experimental.pallas import tpu as pltpu
from jax.sharding import PartitionSpec as P

HD = 128
LANES = 128
CORES = 2
MESH = pl.DeviceIdType.MESH
F32 = jnp.float32
BF16 = jnp.bfloat16


def remote(src, dst, send_sem, recv_sem, where):
    return pltpu.make_async_remote_copy(
        src_ref=src,
        dst_ref=dst,
        send_sem=send_sem,
        recv_sem=recv_sem,
        device_id=where,
        device_id_type=MESH,
    )


def kernel(
    pool_count,
    tp_count,
    chunks,
    cache_len,
    draft_count,
    routes,
    slots,
    route_weights,
    residual_hbm,
    queries_hbm,
    new_kv_hbm,
    cache_hbm,
    out_proj_hbm,
    gain_hbm,
    w_gate_hbm,
    w_up_hbm,
    w_down_hbm,
    out_ref,
    residual,
    queries,
    new_kv,
    cache,
    out_proj,
    gain,
    w_gate,
    w_up,
    w_down,
    attended,
    proj_part,
    proj_in,
    hidden,
    rows_all,
    weights_all,
    gate_acc,
    up_acc,
    act,
    part_all,
    core_in,
    pair_in,
    pair_sum,
    line_in,
    load_sem,
    ps_sem,
    pr_sem,
    wzs_sem,
    wzr_sem,
    wys_sem,
    wyr_sem,
    wc_sem,
    gzs_sem,
    gzr_sem,
    gys_sem,
    gyr_sem,
    gcs_sem,
    gcr_sem,
    szs_sem,
    szr_sem,
    sys_sem,
    syr_sem,
    scs_sem,
    scr_sem,
):
    y_count = pool_count // CORES
    pool_me = lax.axis_index("pool")
    z_me = lax.axis_index("tp")
    y_me = pool_me // CORES
    c_me = lax.rem(pool_me, CORES)
    c_other = 1 - c_me
    core_dev = {"pool": y_me * CORES + c_other}

    def z_at(step):
        return lax.rem(z_me + step, tp_count)

    def y_at(step):
        return lax.rem(y_me + step, y_count)

    def z_dev(z):
        return {"tp": z}

    def y_dev(y):
        return {"pool": y * CORES + c_me}

    rows, dim = residual.shape
    line_rows = tp_count * rows
    half_rows = y_count * line_rows
    all_rows = CORES * half_rows
    width = dim // chunks

    def cols(k):
        return pl.ds(pl.multiple_of(k * width, width), width)

    def row_ds(start, size):
        return pl.ds(pl.multiple_of(start, size), size)

    loads = [
        pltpu.make_async_copy(src, dst, load_sem.at[n])
        for n, (src, dst) in enumerate(
            [
                (queries_hbm, queries),
                (cache_hbm, cache),
                (new_kv_hbm, new_kv),
                (out_proj_hbm, out_proj),
                (residual_hbm, residual),
                (gain_hbm, gain),
                (w_gate_hbm, w_gate),
                (w_up_hbm, w_up),
                (w_down_hbm, w_down),
            ]
        )
    ]
    for load in loads:
        load.start()

    barrier = pltpu.get_barrier_semaphore()
    partners = (
        [core_dev]
        + [y_dev(y_at(s)) for s in range(1, y_count)]
        + [z_dev(z_at(s)) for s in range(1, tp_count)]
    )
    for partner in partners:
        pl.semaphore_signal(barrier, inc=1, device_id=partner, device_id_type=MESH)
    pl.semaphore_wait(barrier, len(partners))

    half_at = c_me * half_rows
    line_at = half_at + y_me * line_rows
    own_at = line_at + z_me * rows

    lanes = weights_all.shape[1]
    expert = lax.broadcasted_iota(jnp.int32, (lanes, rows), 0)
    dense = jnp.zeros((lanes, rows), F32)
    for k in range(routes.shape[0]):
        hit = (routes[k : k + 1, :] == expert) & (slots[k : k + 1, :] >= 0)
        dense = dense + jnp.where(hit, route_weights[k : k + 1, :].astype(F32), 0.0)
    same = lax.broadcasted_iota(jnp.int32, (lanes, lanes), 0) == lax.broadcasted_iota(
        jnp.int32, (lanes, lanes), 1
    )
    tn = (((0,), (0,)), ((), ()))
    weights_all[row_ds(own_at, rows), :] = lax.dot_general(
        dense.astype(BF16), same.astype(F32).astype(BF16), tn, preferred_element_type=F32
    ).astype(BF16)

    def w_z_send(step):
        block = weights_all.at[row_ds(own_at, rows), :]
        z_to = z_at(step)
        return remote(block, block, wzs_sem.at[z_to], wzr_sem.at[z_me], z_dev(z_to))

    def w_z_recv(step):
        z_from = z_at(step)
        block = weights_all.at[row_ds(line_at + z_from * rows, rows), :]
        return remote(block, block, wzs_sem.at[z_from], wzr_sem.at[z_from], z_dev(z_from))

    def w_y_send(step):
        block = weights_all.at[row_ds(line_at, line_rows), :]
        y_to = y_at(step)
        return remote(block, block, wys_sem.at[y_to], wyr_sem.at[y_me], y_dev(y_to))

    def w_y_recv(step):
        y_from = y_at(step)
        block = weights_all.at[row_ds(half_at + y_from * line_rows, line_rows), :]
        return remote(block, block, wys_sem.at[y_from], wyr_sem.at[y_from], y_dev(y_from))

    def w_c_send():
        block = weights_all.at[row_ds(half_at, half_rows), :]
        return remote(block, block, wc_sem.at[0], wc_sem.at[1], core_dev)

    def w_c_recv():
        block = weights_all.at[row_ds(c_other * half_rows, half_rows), :]
        return remote(block, block, wc_sem.at[0], wc_sem.at[1], core_dev)

    for s in range(1, tp_count):
        w_z_send(s).start()

    for load in loads[:3]:
        load.wait()
    requests, cache_size = cache.shape[1], cache.shape[2]
    kv_here = cache.shape[3] // HD
    draft = queries.shape[0] // requests
    group = queries.shape[1] // HD // kv_here
    scale = HD ** (-0.5)
    nt = (((1,), (1,)), ((), ()))
    for r in range(requests):
        span = slice(r * draft, (r + 1) * draft)
        for h in range(kv_here):
            kv_cols = slice(h * HD, (h + 1) * HD)
            q = jnp.concatenate(
                [
                    queries[span, (h * group + g) * HD : (h * group + g + 1) * HD]
                    for g in range(group)
                ],
                axis=0,
            )
            old = lax.dot_general(q, cache[0, r, :, kv_cols], nt, preferred_element_type=F32) * scale
            new = lax.dot_general(q, new_kv[0, span, kv_cols], nt, preferred_element_type=F32) * scale
            old_at = lax.broadcasted_iota(jnp.int32, old.shape, 1)
            new_at = lax.broadcasted_iota(jnp.int32, new.shape, 1)
            new_row = lax.rem(lax.broadcasted_iota(jnp.int32, new.shape, 0), draft)
            see_old = old_at < cache_len[r]
            see_new = (new_at <= new_row) & (new_at < draft_count[r])
            top = jnp.maximum(
                jnp.max(jnp.where(see_old, old, -1e30), axis=1, keepdims=True),
                jnp.max(jnp.where(see_new, new, -1e30), axis=1, keepdims=True),
            )
            p_old = jnp.where(see_old, jnp.exp(old - top), 0.0)
            p_new = jnp.where(see_new, jnp.exp(new - top), 0.0)
            total = jnp.sum(p_old, axis=1, keepdims=True) + jnp.sum(p_new, axis=1, keepdims=True)
            a_old = (p_old / total).astype(BF16)
            a_new = (p_new / total).astype(BF16)
            res = jnp.dot(a_old, cache[1, r, :, kv_cols], preferred_element_type=F32)
            res = res + jnp.dot(a_new, new_kv[1, span, kv_cols], preferred_element_type=F32)
            for g in range(group):
                attended[span, (h * group + g) * HD : (h * group + g + 1) * HD] = res[
                    g * draft : (g + 1) * draft
                ].astype(BF16)

    def proj_send(k, step):
        z_to = z_at(step)
        return remote(
            proj_part.at[row_ds(z_to * rows, rows), cols(k)],
            proj_in.at[z_me, :, cols(k)],
            ps_sem.at[k, z_to],
            pr_sem.at[k, z_me],
            z_dev(z_to),
        )

    def proj_recv(k, step):
        z_from = z_at(step)
        block = proj_in.at[z_from, :, cols(k)]
        return remote(
            proj_part.at[row_ds(z_from * rows, rows), cols(k)],
            block,
            ps_sem.at[k, z_from],
            pr_sem.at[k, z_from],
            z_dev(z_from),
        )

    loads[3].wait()

    def project(k, carry):
        proj_part[:, cols(k)] = jnp.dot(
            attended[...], out_proj[:, cols(k)], preferred_element_type=F32
        ).astype(BF16)
        for s in range(1, tp_count):
            proj_send(k, s).start()
        return carry

    lax.fori_loop(0, chunks, project, 0)

    for s in range(1, tp_count):
        w_z_recv(s).wait_recv()
    for s in range(1, y_count):
        w_y_send(s).start()
    for s in range(1, y_count):
        w_y_recv(s).wait_recv()
    w_c_send().start()

    loads[4].wait()
    loads[5].wait()

    def add_residual(k, power):
        for s in range(1, tp_count):
            proj_recv(k, s).wait_recv()
        total = proj_part[row_ds(z_me * rows, rows), cols(k)].astype(F32)
        for s in range(1, tp_count):
            total = total + proj_in[z_at(s), :, cols(k)].astype(F32)
        h = (residual[:, cols(k)].astype(F32) + total).astype(BF16)
        hidden[:, cols(k)] = h
        wide = h.astype(F32)
        return power + jnp.sum(wide * wide, axis=1, keepdims=True)

    power = lax.fori_loop(0, chunks, add_residual, jnp.zeros((rows, 1), F32))
    factor = lax.rsqrt(power / dim + 1e-05)

    def g_z_send(k, step):
        z_to = z_at(step)
        block = rows_all.at[row_ds(own_at, rows), cols(k)]
        return remote(block, block, gzs_sem.at[k, z_to], gzr_sem.at[k, z_me], z_dev(z_to))

    def g_z_recv(k, step):
        z_from = z_at(step)
        block = rows_all.at[row_ds(line_at + z_from * rows, rows), cols(k)]
        return remote(block, block, gzs_sem.at[k, z_from], gzr_sem.at[k, z_from], z_dev(z_from))

    def g_y_send(k, step):
        y_to = y_at(step)
        block = rows_all.at[row_ds(line_at, line_rows), cols(k)]
        return remote(block, block, gys_sem.at[k, y_to], gyr_sem.at[k, y_me], y_dev(y_to))

    def g_y_recv(k, step):
        y_from = y_at(step)
        block = rows_all.at[row_ds(half_at + y_from * line_rows, line_rows), cols(k)]
        return remote(block, block, gys_sem.at[k, y_from], gyr_sem.at[k, y_from], y_dev(y_from))

    def g_c_send(k):
        block = rows_all.at[row_ds(half_at, half_rows), cols(k)]
        return remote(block, block, gcs_sem.at[k], gcr_sem.at[k], core_dev)

    def g_c_recv(k):
        block = rows_all.at[row_ds(c_other * half_rows, half_rows), cols(k)]
        return remote(block, block, gcs_sem.at[k], gcr_sem.at[k], core_dev)

    def norm(k, carry):
        normed = hidden[:, cols(k)].astype(F32) * factor * gain[:, cols(k)]
        rows_all[row_ds(own_at, rows), cols(k)] = normed.astype(BF16)
        for s in range(1, tp_count):
            g_z_send(k, s).start()
        return carry

    lax.fori_loop(0, chunks, norm, 0)

    gate_acc[...] = jnp.zeros_like(gate_acc)
    up_acc[...] = jnp.zeros_like(up_acc)
    w_c_recv().wait_recv()
    loads[6].wait()
    loads[7].wait()

    def first(i, carry):
        @pl.when(i < chunks)
        def _():
            for s in range(1, tp_count):
                g_z_recv(i, s).wait_recv()
            for s in range(1, y_count):
                g_y_send(i, s).start()

        @pl.when((i >= 1) & (i < chunks + 1))
        def _():
            for s in range(1, y_count):
                g_y_recv(i - 1, s).wait_recv()
            g_c_send(i - 1).start()

        @pl.when(i >= 2)
        def _():
            k = i - 2
            g_c_recv(k).wait_recv()
            block = rows_all[:, cols(k)]
            gate_acc[...] += lax.dot_general(
                block, w_gate[0, :, cols(k)], nt, preferred_element_type=F32
            )
            up_acc[...] += lax.dot_general(
                block, w_up[0, :, cols(k)], nt, preferred_element_type=F32
            )

        return carry

    lax.fori_loop(0, chunks + 2, first, 0)

    gate = gate_acc[...]
    act[...] = (gate / (1.0 + jnp.exp(-gate)) * up_acc[...]).astype(BF16)
    expert_lane = lax.broadcasted_iota(jnp.int32, weights_all.shape, 1) == pool_me
    combine = jnp.sum(
        jnp.where(expert_lane, weights_all[...].astype(F32), 0.0), axis=1, keepdims=True
    )

    def s_c_send(k):
        return remote(
            part_all.at[row_ds(c_other * half_rows, half_rows), cols(k)],
            core_in.at[:, cols(k)],
            scs_sem.at[k],
            scr_sem.at[k],
            core_dev,
        )

    def s_y_send(k, step):
        y_to = y_at(step)
        return remote(
            core_in.at[row_ds(y_to * line_rows, line_rows), cols(k)],
            pair_in.at[y_me, :, cols(k)],
            sys_sem.at[k, y_to],
            syr_sem.at[k, y_me],
            y_dev(y_to),
        )

    def s_y_recv(k, step):
        y_from = y_at(step)
        return remote(
            core_in.at[row_ds(y_from * line_rows, line_rows), cols(k)],
            pair_in.at[y_from, :, cols(k)],
            sys_sem.at[k, y_from],
            syr_sem.at[k, y_from],
            y_dev(y_from),
        )

    def s_z_send(k, step):
        z_to = z_at(step)
        return remote(
            pair_sum.at[row_ds(z_to * rows, rows), cols(k)],
            line_in.at[z_me, :, cols(k)],
            szs_sem.at[k, z_to],
            szr_sem.at[k, z_me],
            z_dev(z_to),
        )

    def s_z_recv(k, step):
        z_from = z_at(step)
        return remote(
            pair_sum.at[row_ds(z_from * rows, rows), cols(k)],
            line_in.at[z_from, :, cols(k)],
            szs_sem.at[k, z_from],
            szr_sem.at[k, z_from],
            z_dev(z_from),
        )

    loads[8].wait()

    def second(i, carry):
        @pl.when(i < chunks)
        def _():
            part = jnp.dot(act[...], w_down[0, :, cols(i)], preferred_element_type=F32)
            part_all[:, cols(i)] = (part * combine).astype(BF16)
            s_c_send(i).start()

        @pl.when((i >= 1) & (i < chunks + 1))
        def _():
            k = i - 1
            s_c_send(k).wait_recv()
            core_in[:, cols(k)] = (
                core_in[:, cols(k)].astype(F32)
                + part_all[row_ds(half_at, half_rows), cols(k)].astype(F32)
            ).astype(BF16)
            for s in range(1, y_count):
                s_y_send(k, s).start()

        @pl.when((i >= 2) & (i < chunks + 2))
        def _():
            k = i - 2
            total = core_in[row_ds(y_me * line_rows, line_rows), cols(k)].astype(F32)
            for s in range(1, y_count):
                s_y_recv(k, s).wait_recv()
                total = total + pair_in[y_at(s), :, cols(k)].astype(F32)
            pair_sum[:, cols(k)] = total.astype(BF16)
            for s in range(1, tp_count):
                s_z_send(k, s).start()

        @pl.when(i >= 3)
        def _():
            k = i - 3
            total = pair_sum[row_ds(z_me * rows, rows), cols(k)].astype(F32)
            for s in range(1, tp_count):
                s_z_recv(k, s).wait_recv()
                total = total + line_in[z_at(s), :, cols(k)].astype(F32)
            out_ref[:, cols(k)] = (hidden[:, cols(k)].astype(F32) + total).astype(BF16)

        return carry

    lax.fori_loop(0, chunks + 3, second, 0)

    for s in range(1, tp_count):
        w_z_send(s).wait_send()
    for s in range(1, y_count):
        w_y_send(s).wait_send()
    w_c_send().wait_send()

    def drain(k, carry):
        for s in range(1, tp_count):
            proj_send(k, s).wait_send()
            g_z_send(k, s).wait_send()
            s_z_send(k, s).wait_send()
        for s in range(1, y_count):
            g_y_send(k, s).wait_send()
            s_y_send(k, s).wait_send()
        g_c_send(k).wait_send()
        s_c_send(k).wait_send()
        return carry

    lax.fori_loop(0, chunks, drain, 0)


def local(
    pool_count,
    tp_count,
    residual,
    queries,
    new_kv,
    cache,
    cache_len,
    draft_count,
    out_proj,
    norm_gain,
    routes,
    slots,
    route_weights,
    w_gate,
    w_up,
    w_down,
):
    rows, dim = residual.shape
    y_count = pool_count // CORES
    line_rows = tp_count * rows
    half_rows = y_count * line_rows
    all_rows = CORES * half_rows
    hidden_units = w_down.shape[1]
    weight_lanes = pl.cdiv(pool_count, LANES) * LANES
    chunks = 4
    gain = norm_gain.reshape(1, dim)
    w_gate, w_up = jnp.swapaxes(w_gate, 1, 2), jnp.swapaxes(w_up, 1, 2)
    routes, slots, route_weights = routes.T, slots.T, route_weights.T
    dma = pltpu.SemaphoreType.DMA
    loaded = (residual, queries, new_kv, cache, out_proj, gain, w_gate, w_up, w_down)
    smem = pl.BlockSpec(memory_space=pltpu.SMEM)
    vmem = pl.BlockSpec(memory_space=pltpu.VMEM)
    return pl.pallas_call(
        functools.partial(kernel, pool_count, tp_count, chunks),
        out_shape=jax.ShapeDtypeStruct((rows, dim), BF16),
        in_specs=[smem] * 2 + [vmem] * 3 + [pl.BlockSpec(memory_space=pl.ANY)] * len(loaded),
        out_specs=vmem,
        scratch_shapes=[pltpu.VMEM(a.shape, a.dtype) for a in loaded]
        + [
            pltpu.VMEM((queries.shape[0], queries.shape[1]), BF16),
            pltpu.VMEM((line_rows, dim), BF16),
            pltpu.VMEM((tp_count, rows, dim), BF16),
            pltpu.VMEM((rows, dim), BF16),
            pltpu.VMEM((all_rows, dim), BF16),
            pltpu.VMEM((all_rows, weight_lanes), BF16),
            pltpu.VMEM((all_rows, hidden_units), F32),
            pltpu.VMEM((all_rows, hidden_units), F32),
            pltpu.VMEM((all_rows, hidden_units), BF16),
            pltpu.VMEM((all_rows, dim), BF16),
            pltpu.VMEM((half_rows, dim), BF16),
            pltpu.VMEM((y_count, line_rows, dim), BF16),
            pltpu.VMEM((line_rows, dim), BF16),
            pltpu.VMEM((tp_count, rows, dim), BF16),
            dma((len(loaded),)),
            dma((chunks, tp_count)),
            dma((chunks, tp_count)),
            dma((tp_count,)),
            dma((tp_count,)),
            dma((y_count,)),
            dma((y_count,)),
            dma((2,)),
            dma((chunks, tp_count)),
            dma((chunks, tp_count)),
            dma((chunks, y_count)),
            dma((chunks, y_count)),
            dma((chunks,)),
            dma((chunks,)),
            dma((chunks, tp_count)),
            dma((chunks, tp_count)),
            dma((chunks, y_count)),
            dma((chunks, y_count)),
            dma((chunks,)),
            dma((chunks,)),
        ],
        compiler_params=pltpu.CompilerParams(
            collective_id=0, has_side_effects=True, vmem_limit_bytes=60 * 1024 * 1024
        ),
    )(cache_len, draft_count, routes, slots, route_weights, *loaded)


def solution(mesh):
    in_specs = (
        P(("parts", "pool", "tp"), None),
        P(("parts", "pool"), "tp"),
        P(None, ("parts", "pool"), "tp"),
        P(None, ("parts", "pool"), None, "tp"),
        P(("parts", "pool")),
        P(("parts", "pool")),
        P("tp", None),
        P(),
        P(("parts", "pool", "tp"), None),
        P(("parts", "pool", "tp"), None),
        P(("parts", "pool", "tp"), None),
        P("pool", None, "tp"),
        P("pool", None, "tp"),
        P("pool", "tp", None),
    )
    out_specs = P(("parts", "pool", "tp"), None)
    body = functools.partial(local, mesh.shape["pool"], mesh.shape["tp"])
    return jax.shard_map(body, mesh=mesh, in_specs=in_specs, out_specs=out_specs, check_vma=False)
```

```python
import functools

import jax
import jax.numpy as jnp
from jax import lax
from jax.experimental import pallas as pl
from jax.experimental.pallas import tpu as pltpu
from jax.sharding import PartitionSpec as P

HD = 128
LANES = 128
CORES = 2
MESH = pl.DeviceIdType.MESH
F32 = jnp.float32
BF16 = jnp.bfloat16


def remote(src, dst, send_sem, recv_sem, where):
    return pltpu.make_async_remote_copy(
        src_ref=src,
        dst_ref=dst,
        send_sem=send_sem,
        recv_sem=recv_sem,
        device_id=where,
        device_id_type=MESH,
    )


def kernel(
    pool_count,
    tp_count,
    chunks,
    lag,
    cache_len,
    draft_count,
    routes,
    slots,
    route_weights,
    residual_hbm,
    queries_hbm,
    new_kv_hbm,
    cache_hbm,
    out_proj_hbm,
    gain_hbm,
    w_gate_hbm,
    w_up_hbm,
    w_down_hbm,
    out_ref,
    residual,
    queries,
    new_kv,
    cache,
    out_proj,
    gain,
    w_gate,
    w_up,
    w_down,
    attended,
    proj_part,
    proj_in,
    hidden,
    rows_all,
    weights_all,
    power,
    gate_acc,
    up_acc,
    act,
    part_all,
    core_in,
    pair_in,
    pair_sum,
    line_in,
    load_sem,
    ps_sem,
    pr_sem,
    wzs_sem,
    wzr_sem,
    wys_sem,
    wyr_sem,
    wc_sem,
    gzs_sem,
    gzr_sem,
    gys_sem,
    gyr_sem,
    gcs_sem,
    gcr_sem,
    szs_sem,
    szr_sem,
    sys_sem,
    syr_sem,
    scs_sem,
    scr_sem,
):
    y_count = pool_count // CORES
    pool_me = lax.axis_index("pool")
    z_me = lax.axis_index("tp")
    y_me = pool_me // CORES
    c_me = lax.rem(pool_me, CORES)
    c_other = 1 - c_me
    core_dev = {"pool": y_me * CORES + c_other}

    def z_at(step):
        return lax.rem(z_me + step, tp_count)

    def y_at(step):
        return lax.rem(y_me + step, y_count)

    def z_dev(z):
        return {"tp": z}

    def y_dev(y):
        return {"pool": y * CORES + c_me}

    rows, dim = residual.shape
    line_rows = tp_count * rows
    half_rows = y_count * line_rows
    all_rows = CORES * half_rows
    width = dim // chunks

    def cols(k):
        return pl.ds(pl.multiple_of(k * width, width), width)

    def row_ds(start, size):
        return pl.ds(pl.multiple_of(start, size), size)

    loads = [
        pltpu.make_async_copy(src, dst, load_sem.at[n])
        for n, (src, dst) in enumerate(
            [
                (queries_hbm, queries),
                (cache_hbm, cache),
                (new_kv_hbm, new_kv),
                (out_proj_hbm, out_proj),
                (residual_hbm, residual),
                (gain_hbm, gain),
                (w_gate_hbm, w_gate),
                (w_up_hbm, w_up),
                (w_down_hbm, w_down),
            ]
        )
    ]
    for load in loads[:6]:
        load.start()

    barrier = pltpu.get_barrier_semaphore()
    partners = (
        [core_dev]
        + [y_dev(y_at(s)) for s in range(1, y_count)]
        + [z_dev(z_at(s)) for s in range(1, tp_count)]
    )
    for partner in partners:
        pl.semaphore_signal(barrier, inc=1, device_id=partner, device_id_type=MESH)
    half_at = c_me * half_rows
    line_at = half_at + y_me * line_rows
    own_at = line_at + z_me * rows

    def w_z_send(step):
        block = weights_all.at[row_ds(own_at, rows), :]
        z_to = z_at(step)
        return remote(block, block, wzs_sem.at[z_to], wzr_sem.at[z_me], z_dev(z_to))

    def w_z_recv(step):
        z_from = z_at(step)
        block = weights_all.at[row_ds(line_at + z_from * rows, rows), :]
        return remote(block, block, wzs_sem.at[z_from], wzr_sem.at[z_from], z_dev(z_from))

    def w_y_send(step):
        block = weights_all.at[row_ds(line_at, line_rows), :]
        y_to = y_at(step)
        return remote(block, block, wys_sem.at[y_to], wyr_sem.at[y_me], y_dev(y_to))

    def w_y_recv(step):
        y_from = y_at(step)
        block = weights_all.at[row_ds(half_at + y_from * line_rows, line_rows), :]
        return remote(block, block, wys_sem.at[y_from], wyr_sem.at[y_from], y_dev(y_from))

    def w_c_send():
        block = weights_all.at[row_ds(half_at, half_rows), :]
        return remote(block, block, wc_sem.at[0], wc_sem.at[1], core_dev)

    def w_c_recv():
        block = weights_all.at[row_ds(c_other * half_rows, half_rows), :]
        return remote(block, block, wc_sem.at[0], wc_sem.at[1], core_dev)

    for load in loads[:3]:
        load.wait()
    requests, cache_size = cache.shape[1], cache.shape[2]
    kv_here = cache.shape[3] // HD
    draft = queries.shape[0] // requests
    group = queries.shape[1] // HD // kv_here
    scale = HD ** (-0.5)
    nt = (((1,), (1,)), ((), ()))
    for r in range(requests):
        span = slice(r * draft, (r + 1) * draft)
        for h in range(kv_here):
            kv_cols = slice(h * HD, (h + 1) * HD)
            q = jnp.concatenate(
                [
                    queries[span, (h * group + g) * HD : (h * group + g + 1) * HD]
                    for g in range(group)
                ],
                axis=0,
            )
            old = lax.dot_general(q, cache[0, r, :, kv_cols], nt, preferred_element_type=F32) * scale
            new = lax.dot_general(q, new_kv[0, span, kv_cols], nt, preferred_element_type=F32) * scale
            old_at = lax.broadcasted_iota(jnp.int32, old.shape, 1)
            new_at = lax.broadcasted_iota(jnp.int32, new.shape, 1)
            new_row = lax.rem(lax.broadcasted_iota(jnp.int32, new.shape, 0), draft)
            see_old = old_at < cache_len[r]
            see_new = (new_at <= new_row) & (new_at < draft_count[r])
            top = jnp.maximum(
                jnp.max(jnp.where(see_old, old, -1e30), axis=1, keepdims=True),
                jnp.max(jnp.where(see_new, new, -1e30), axis=1, keepdims=True),
            )
            p_old = jnp.where(see_old, jnp.exp(old - top), 0.0)
            p_new = jnp.where(see_new, jnp.exp(new - top), 0.0)
            total = jnp.sum(p_old, axis=1, keepdims=True) + jnp.sum(p_new, axis=1, keepdims=True)
            a_old = (p_old / total).astype(BF16)
            a_new = (p_new / total).astype(BF16)
            res = jnp.dot(a_old, cache[1, r, :, kv_cols], preferred_element_type=F32)
            res = res + jnp.dot(a_new, new_kv[1, span, kv_cols], preferred_element_type=F32)
            for g in range(group):
                attended[span, (h * group + g) * HD : (h * group + g + 1) * HD] = res[
                    g * draft : (g + 1) * draft
                ].astype(BF16)

    def proj_send(k, step):
        z_to = z_at(step)
        return remote(
            proj_part.at[k, row_ds(z_to * rows, rows), :],
            proj_in.at[k, z_me],
            ps_sem.at[k, z_to],
            pr_sem.at[k, z_me],
            z_dev(z_to),
        )

    def proj_recv(k, step):
        z_from = z_at(step)
        block = proj_in.at[k, z_from]
        return remote(
            proj_part.at[k, row_ds(z_from * rows, rows), :],
            block,
            ps_sem.at[k, z_from],
            pr_sem.at[k, z_from],
            z_dev(z_from),
        )

    lanes = weights_all.shape[1]
    expert = lax.broadcasted_iota(jnp.int32, (lanes, rows), 0)
    dense = jnp.zeros((lanes, rows), F32)
    for k in range(routes.shape[0]):
        hit = (routes[k : k + 1, :] == expert) & (slots[k : k + 1, :] >= 0)
        dense = dense + jnp.where(hit, route_weights[k : k + 1, :].astype(F32), 0.0)
    same = lax.broadcasted_iota(jnp.int32, (lanes, lanes), 0) == lax.broadcasted_iota(
        jnp.int32, (lanes, lanes), 1
    )
    tn = (((0,), (0,)), ((), ()))
    weights_all[row_ds(own_at, rows), :] = lax.dot_general(
        dense.astype(BF16), same.astype(F32).astype(BF16), tn, preferred_element_type=F32
    )

    loads[3].wait()
    for load in loads[6:]:
        load.start()

    pl.semaphore_wait(barrier, len(partners))

    def project(k, carry):
        proj_part[k] = jnp.dot(
            attended[...], out_proj[:, cols(k)], preferred_element_type=F32
        ).astype(BF16)
        for s in range(1, tp_count):
            proj_send(k, s).start()
        return carry

    lax.fori_loop(0, chunks, project, 0)

    loads[4].wait()
    loads[5].wait()

    def g_z_send(k, step):
        z_to = z_at(step)
        block = rows_all.at[k, row_ds(own_at, rows), :]
        return remote(block, block, gzs_sem.at[k, z_to], gzr_sem.at[k, z_me], z_dev(z_to))

    def g_z_recv(k, step):
        z_from = z_at(step)
        block = rows_all.at[k, row_ds(line_at + z_from * rows, rows), :]
        return remote(block, block, gzs_sem.at[k, z_from], gzr_sem.at[k, z_from], z_dev(z_from))

    def g_y_send(k, step):
        y_to = y_at(step)
        block = rows_all.at[k, row_ds(line_at, line_rows), :]
        return remote(block, block, gys_sem.at[k, y_to], gyr_sem.at[k, y_me], y_dev(y_to))

    def g_y_recv(k, step):
        y_from = y_at(step)
        block = rows_all.at[k, row_ds(half_at + y_from * line_rows, line_rows), :]
        return remote(block, block, gys_sem.at[k, y_from], gyr_sem.at[k, y_from], y_dev(y_from))

    def g_c_send(k):
        block = rows_all.at[k, row_ds(half_at, half_rows), :]
        return remote(block, block, gcs_sem.at[k], gcr_sem.at[k], core_dev)

    def g_c_recv(k):
        block = rows_all.at[k, row_ds(c_other * half_rows, half_rows), :]
        return remote(block, block, gcs_sem.at[k], gcr_sem.at[k], core_dev)

    gate_acc[...] = jnp.zeros_like(gate_acc)
    up_acc[...] = jnp.zeros_like(up_acc)
    power[...] = jnp.zeros_like(power)
    loads[6].wait()
    loads[7].wait()

    def first(i, carry):
        @pl.when(i < chunks)
        def _():
            for s in range(1, tp_count):
                proj_recv(i, s).wait_recv()
            total = proj_part[i, row_ds(z_me * rows, rows), :].astype(F32)
            for s in range(1, tp_count):
                total = total + proj_in[i, z_at(s)].astype(F32)
            h = (residual[:, cols(i)].astype(F32) + total).astype(BF16)
            hidden[:, cols(i)] = h
            wide = h.astype(F32)
            rows_all[i, row_ds(own_at, rows), :] = (wide * gain[:, cols(i)]).astype(BF16)
            for s in range(1, tp_count):
                g_z_send(i, s).start()
            power[...] += jnp.sum(wide * wide, axis=1, keepdims=True)

        @pl.when(i == chunks)
        def _():
            factor = lax.rsqrt(power[...] / dim + 1e-05)
            own = weights_all[row_ds(own_at, rows), :]
            at = lax.broadcasted_iota(jnp.int32, own.shape, 1)
            weights_all[row_ds(own_at, rows), :] = jnp.where(at == pool_count, factor, own)
            for s in range(1, tp_count):
                w_z_send(s).start()

        @pl.when((i >= lag) & (i < chunks + lag))
        def _():
            k = i - lag
            for s in range(1, tp_count):
                g_z_recv(k, s).wait_recv()
            for s in range(1, y_count):
                g_y_send(k, s).start()

        @pl.when(i == chunks + lag)
        def _():
            for s in range(1, tp_count):
                w_z_recv(s).wait_recv()
            for s in range(1, y_count):
                w_y_send(s).start()

        @pl.when((i >= 2 * lag) & (i < chunks + 2 * lag))
        def _():
            k = i - 2 * lag
            for s in range(1, y_count):
                g_y_recv(k, s).wait_recv()
            g_c_send(k).start()

        @pl.when(i == chunks + 2 * lag)
        def _():
            for s in range(1, y_count):
                w_y_recv(s).wait_recv()
            w_c_send().start()

        @pl.when(i >= 3 * lag)
        def _():
            k = i - 3 * lag
            g_c_recv(k).wait_recv()
            block = rows_all[k]
            gate_acc[...] += lax.dot_general(
                block, w_gate[0, :, cols(k)], nt, preferred_element_type=F32
            )
            up_acc[...] += lax.dot_general(
                block, w_up[0, :, cols(k)], nt, preferred_element_type=F32
            )

        return carry

    lax.fori_loop(0, chunks + 3 * lag, first, 0)
    w_c_recv().wait_recv()

    def column(at):
        lane = lax.broadcasted_iota(jnp.int32, weights_all.shape, 1)
        return jnp.sum(jnp.where(lane == at, weights_all[...], 0.0), axis=1, keepdims=True)

    factor_all = column(pool_count)
    combine = column(pool_me)
    gate = gate_acc[...] * factor_all
    act[...] = (gate / (1.0 + jnp.exp(-gate)) * (up_acc[...] * factor_all)).astype(BF16)

    def s_c_send(k):
        return remote(
            part_all.at[k, row_ds(c_other * half_rows, half_rows), :],
            core_in.at[k],
            scs_sem.at[k],
            scr_sem.at[k],
            core_dev,
        )

    def s_y_send(k, step):
        y_to = y_at(step)
        return remote(
            core_in.at[k, row_ds(y_to * line_rows, line_rows), :],
            pair_in.at[k, y_me],
            sys_sem.at[k, y_to],
            syr_sem.at[k, y_me],
            y_dev(y_to),
        )

    def s_y_recv(k, step):
        y_from = y_at(step)
        return remote(
            core_in.at[k, row_ds(y_from * line_rows, line_rows), :],
            pair_in.at[k, y_from],
            sys_sem.at[k, y_from],
            syr_sem.at[k, y_from],
            y_dev(y_from),
        )

    def s_z_send(k, step):
        z_to = z_at(step)
        return remote(
            pair_sum.at[k, row_ds(z_to * rows, rows), :],
            line_in.at[k, z_me],
            szs_sem.at[k, z_to],
            szr_sem.at[k, z_me],
            z_dev(z_to),
        )

    def s_z_recv(k, step):
        z_from = z_at(step)
        return remote(
            pair_sum.at[k, row_ds(z_from * rows, rows), :],
            line_in.at[k, z_from],
            szs_sem.at[k, z_from],
            szr_sem.at[k, z_from],
            z_dev(z_from),
        )

    loads[8].wait()

    def second(i, carry):
        @pl.when(i < chunks)
        def _():
            part = jnp.dot(act[...], w_down[0, :, cols(i)], preferred_element_type=F32)
            part_all[i] = (part * combine).astype(BF16)
            s_c_send(i).start()

        @pl.when((i >= lag) & (i < chunks + lag))
        def _():
            k = i - lag
            s_c_send(k).wait_recv()
            core_in[k] = (
                core_in[k].astype(F32)
                + part_all[k, row_ds(half_at, half_rows), :].astype(F32)
            ).astype(BF16)
            for s in range(1, y_count):
                s_y_send(k, s).start()

        @pl.when((i >= 2 * lag) & (i < chunks + 2 * lag))
        def _():
            k = i - 2 * lag
            total = core_in[k, row_ds(y_me * line_rows, line_rows), :].astype(F32)
            for s in range(1, y_count):
                s_y_recv(k, s).wait_recv()
                total = total + pair_in[k, y_at(s)].astype(F32)
            pair_sum[k] = total.astype(BF16)
            for s in range(1, tp_count):
                s_z_send(k, s).start()

        @pl.when(i >= 3 * lag)
        def _():
            k = i - 3 * lag
            total = pair_sum[k, row_ds(z_me * rows, rows), :].astype(F32)
            for s in range(1, tp_count):
                s_z_recv(k, s).wait_recv()
                total = total + line_in[k, z_at(s)].astype(F32)
            out_ref[:, cols(k)] = (hidden[:, cols(k)].astype(F32) + total).astype(BF16)

        return carry

    lax.fori_loop(0, chunks + 3 * lag, second, 0)

    for s in range(1, tp_count):
        w_z_send(s).wait_send()
    for s in range(1, y_count):
        w_y_send(s).wait_send()
    w_c_send().wait_send()

    def drain(k, carry):
        for s in range(1, tp_count):
            proj_send(k, s).wait_send()
            g_z_send(k, s).wait_send()
            s_z_send(k, s).wait_send()
        for s in range(1, y_count):
            g_y_send(k, s).wait_send()
            s_y_send(k, s).wait_send()
        g_c_send(k).wait_send()
        s_c_send(k).wait_send()
        return carry

    lax.fori_loop(0, chunks, drain, 0)


def local(
    pool_count,
    tp_count,
    residual,
    queries,
    new_kv,
    cache,
    cache_len,
    draft_count,
    out_proj,
    norm_gain,
    routes,
    slots,
    route_weights,
    w_gate,
    w_up,
    w_down,
):
    rows, dim = residual.shape
    y_count = pool_count // CORES
    line_rows = tp_count * rows
    half_rows = y_count * line_rows
    all_rows = CORES * half_rows
    hidden_units = w_down.shape[1]
    weight_lanes = pl.cdiv(pool_count + 1, LANES) * LANES
    chunks, lag = 8, 3
    width = dim // chunks
    gain = norm_gain.reshape(1, dim)
    w_gate, w_up = jnp.swapaxes(w_gate, 1, 2), jnp.swapaxes(w_up, 1, 2)
    routes, slots, route_weights = routes.T, slots.T, route_weights.T
    dma = pltpu.SemaphoreType.DMA
    loaded = (residual, queries, new_kv, cache, out_proj, gain, w_gate, w_up, w_down)
    smem = pl.BlockSpec(memory_space=pltpu.SMEM)
    vmem = pl.BlockSpec(memory_space=pltpu.VMEM)
    return pl.pallas_call(
        functools.partial(kernel, pool_count, tp_count, chunks, lag),
        out_shape=jax.ShapeDtypeStruct((rows, dim), BF16),
        in_specs=[smem] * 2 + [vmem] * 3 + [pl.BlockSpec(memory_space=pl.ANY)] * len(loaded),
        out_specs=vmem,
        scratch_shapes=[pltpu.VMEM(a.shape, a.dtype) for a in loaded]
        + [
            pltpu.VMEM((queries.shape[0], queries.shape[1]), BF16),
            pltpu.VMEM((chunks, line_rows, width), BF16),
            pltpu.VMEM((chunks, tp_count, rows, width), BF16),
            pltpu.VMEM((rows, dim), BF16),
            pltpu.VMEM((chunks, all_rows, width), BF16),
            pltpu.VMEM((all_rows, weight_lanes), F32),
            pltpu.VMEM((rows, weight_lanes), F32),
            pltpu.VMEM((all_rows, hidden_units), F32),
            pltpu.VMEM((all_rows, hidden_units), F32),
            pltpu.VMEM((all_rows, hidden_units), BF16),
            pltpu.VMEM((chunks, all_rows, width), BF16),
            pltpu.VMEM((chunks, half_rows, width), BF16),
            pltpu.VMEM((chunks, y_count, line_rows, width), BF16),
            pltpu.VMEM((chunks, line_rows, width), BF16),
            pltpu.VMEM((chunks, tp_count, rows, width), BF16),
            dma((len(loaded),)),
            dma((chunks, tp_count)),
            dma((chunks, tp_count)),
            dma((tp_count,)),
            dma((tp_count,)),
            dma((y_count,)),
            dma((y_count,)),
            dma((2,)),
            dma((chunks, tp_count)),
            dma((chunks, tp_count)),
            dma((chunks, y_count)),
            dma((chunks, y_count)),
            dma((chunks,)),
            dma((chunks,)),
            dma((chunks, tp_count)),
            dma((chunks, tp_count)),
            dma((chunks, y_count)),
            dma((chunks, y_count)),
            dma((chunks,)),
            dma((chunks,)),
        ],
        compiler_params=pltpu.CompilerParams(
            collective_id=0, has_side_effects=True, vmem_limit_bytes=60 * 1024 * 1024
        ),
    )(cache_len, draft_count, routes, slots, route_weights, *loaded)


def solution(mesh):
    in_specs = (
        P(("parts", "pool", "tp"), None),
        P(("parts", "pool"), "tp"),
        P(None, ("parts", "pool"), "tp"),
        P(None, ("parts", "pool"), None, "tp"),
        P(("parts", "pool")),
        P(("parts", "pool")),
        P("tp", None),
        P(),
        P(("parts", "pool", "tp"), None),
        P(("parts", "pool", "tp"), None),
        P(("parts", "pool", "tp"), None),
        P("pool", None, "tp"),
        P("pool", None, "tp"),
        P("pool", "tp", None),
    )
    out_specs = P(("parts", "pool", "tp"), None)
    body = functools.partial(local, mesh.shape["pool"], mesh.shape["tp"])
    return jax.shard_map(body, mesh=mesh, in_specs=in_specs, out_specs=out_specs, check_vma=False)
```

```python
import functools

import jax
import jax.numpy as jnp
from jax import lax
from jax.experimental import pallas as pl
from jax.experimental.pallas import tpu as pltpu
from jax.sharding import PartitionSpec as P

HD = 128
LANES = 128
CORES = 2
MESH = pl.DeviceIdType.MESH
F32 = jnp.float32
BF16 = jnp.bfloat16


def remote(src, dst, send_sem, recv_sem, where):
    return pltpu.make_async_remote_copy(
        src_ref=src,
        dst_ref=dst,
        send_sem=send_sem,
        recv_sem=recv_sem,
        device_id=where,
        device_id_type=MESH,
    )


def kernel(
    pool_count,
    tp_count,
    chunks,
    lag,
    cache_len,
    draft_count,
    routes,
    slots,
    route_weights,
    residual_hbm,
    queries_hbm,
    new_kv_hbm,
    cache_hbm,
    out_proj_hbm,
    gain_hbm,
    w_gate_hbm,
    w_up_hbm,
    w_down_hbm,
    out_ref,
    residual,
    queries,
    new_kv,
    cache,
    out_proj,
    gain,
    w_gate,
    w_up,
    w_down,
    attended,
    proj_part,
    proj_in,
    hidden,
    rows_all,
    weights_all,
    power,
    gate_acc,
    up_acc,
    act,
    part_all,
    core_in,
    pair_in,
    pair_sum,
    line_in,
    load_sem,
    ps_sem,
    pr_sem,
    wzs_sem,
    wzr_sem,
    wys_sem,
    wyr_sem,
    wc_sem,
    gzs_sem,
    gzr_sem,
    gys_sem,
    gyr_sem,
    gcs_sem,
    gcr_sem,
    szs_sem,
    szr_sem,
    sys_sem,
    syr_sem,
    scs_sem,
    scr_sem,
):
    y_count = pool_count // CORES
    pool_me = lax.axis_index("pool")
    z_me = lax.axis_index("tp")
    y_me = pool_me // CORES
    c_me = lax.rem(pool_me, CORES)
    c_other = 1 - c_me
    core_dev = {"pool": y_me * CORES + c_other}

    def z_at(step):
        return lax.rem(z_me + step, tp_count)

    def y_at(step):
        return lax.rem(y_me + step, y_count)

    def z_dev(z):
        return {"tp": z}

    def y_dev(y):
        return {"pool": y * CORES + c_me}

    rows, dim = residual.shape
    line_rows = tp_count * rows
    half_rows = y_count * line_rows
    all_rows = CORES * half_rows
    width = dim // chunks

    def cols(k):
        return pl.ds(pl.multiple_of(k * width, width), width)

    def row_ds(start, size):
        return pl.ds(pl.multiple_of(start, size), size)

    loads = [
        pltpu.make_async_copy(src, dst, load_sem.at[n])
        for n, (src, dst) in enumerate(
            [
                (queries_hbm, queries),
                (cache_hbm, cache),
                (new_kv_hbm, new_kv),
                (out_proj_hbm, out_proj),
                (residual_hbm, residual),
                (gain_hbm, gain),
                (w_gate_hbm, w_gate),
                (w_up_hbm, w_up),
                (w_down_hbm, w_down),
            ]
        )
    ]
    for load in loads[:6]:
        load.start()

    barrier = pltpu.get_barrier_semaphore()
    partners = (
        [core_dev]
        + [y_dev(y_at(s)) for s in range(1, y_count)]
        + [z_dev(z_at(s)) for s in range(1, tp_count)]
    )
    for partner in partners:
        pl.semaphore_signal(barrier, inc=1, device_id=partner, device_id_type=MESH)
    half_at = c_me * half_rows
    line_at = half_at + y_me * line_rows
    own_at = line_at + z_me * rows

    def w_z_send(step):
        block = weights_all.at[row_ds(own_at, rows), :]
        z_to = z_at(step)
        return remote(block, block, wzs_sem.at[z_to], wzr_sem.at[z_me], z_dev(z_to))

    def w_z_recv(step):
        z_from = z_at(step)
        block = weights_all.at[row_ds(line_at + z_from * rows, rows), :]
        return remote(block, block, wzs_sem.at[z_from], wzr_sem.at[z_from], z_dev(z_from))

    def w_y_send(step):
        block = weights_all.at[row_ds(line_at, line_rows), :]
        y_to = y_at(step)
        return remote(block, block, wys_sem.at[y_to], wyr_sem.at[y_me], y_dev(y_to))

    def w_y_recv(step):
        y_from = y_at(step)
        block = weights_all.at[row_ds(half_at + y_from * line_rows, line_rows), :]
        return remote(block, block, wys_sem.at[y_from], wyr_sem.at[y_from], y_dev(y_from))

    def w_c_send():
        block = weights_all.at[row_ds(half_at, half_rows), :]
        return remote(block, block, wc_sem.at[0], wc_sem.at[1], core_dev)

    def w_c_recv():
        block = weights_all.at[row_ds(c_other * half_rows, half_rows), :]
        return remote(block, block, wc_sem.at[0], wc_sem.at[1], core_dev)

    for load in loads[:3]:
        load.wait()
    requests, cache_size = cache.shape[1], cache.shape[2]
    kv_here = cache.shape[3] // HD
    draft = queries.shape[0] // requests
    group = queries.shape[1] // HD // kv_here
    scale = HD ** (-0.5)
    nt = (((1,), (1,)), ((), ()))
    for r in range(requests):
        span = slice(r * draft, (r + 1) * draft)
        for h in range(kv_here):
            kv_cols = slice(h * HD, (h + 1) * HD)
            q = jnp.concatenate(
                [
                    queries[span, (h * group + g) * HD : (h * group + g + 1) * HD]
                    for g in range(group)
                ],
                axis=0,
            )
            old = lax.dot_general(q, cache[0, r, :, kv_cols], nt, preferred_element_type=F32) * scale
            new = lax.dot_general(q, new_kv[0, span, kv_cols], nt, preferred_element_type=F32) * scale
            old_at = lax.broadcasted_iota(jnp.int32, old.shape, 1)
            new_at = lax.broadcasted_iota(jnp.int32, new.shape, 1)
            new_row = lax.rem(lax.broadcasted_iota(jnp.int32, new.shape, 0), draft)
            see_old = old_at < cache_len[r]
            see_new = (new_at <= new_row) & (new_at < draft_count[r])
            top = jnp.maximum(
                jnp.max(jnp.where(see_old, old, -1e30), axis=1, keepdims=True),
                jnp.max(jnp.where(see_new, new, -1e30), axis=1, keepdims=True),
            )
            p_old = jnp.where(see_old, jnp.exp(old - top), 0.0)
            p_new = jnp.where(see_new, jnp.exp(new - top), 0.0)
            total = jnp.sum(p_old, axis=1, keepdims=True) + jnp.sum(p_new, axis=1, keepdims=True)
            a_old = (p_old / total).astype(BF16)
            a_new = (p_new / total).astype(BF16)
            res = jnp.dot(a_old, cache[1, r, :, kv_cols], preferred_element_type=F32)
            res = res + jnp.dot(a_new, new_kv[1, span, kv_cols], preferred_element_type=F32)
            for g in range(group):
                attended[span, (h * group + g) * HD : (h * group + g + 1) * HD] = res[
                    g * draft : (g + 1) * draft
                ].astype(BF16)

    def proj_send(k, step):
        z_to = z_at(step)
        return remote(
            proj_part.at[k, row_ds(z_to * rows, rows), :],
            proj_in.at[k, z_me],
            ps_sem.at[k, z_to],
            pr_sem.at[k, z_me],
            z_dev(z_to),
        )

    def proj_recv(k, step):
        z_from = z_at(step)
        block = proj_in.at[k, z_from]
        return remote(
            proj_part.at[k, row_ds(z_from * rows, rows), :],
            block,
            ps_sem.at[k, z_from],
            pr_sem.at[k, z_from],
            z_dev(z_from),
        )

    lanes = weights_all.shape[1]
    expert = lax.broadcasted_iota(jnp.int32, (lanes, rows), 0)
    dense = jnp.zeros((lanes, rows), F32)
    for k in range(routes.shape[0]):
        hit = (routes[k : k + 1, :] == expert) & (slots[k : k + 1, :] >= 0)
        dense = dense + jnp.where(hit, route_weights[k : k + 1, :].astype(F32), 0.0)
    same = lax.broadcasted_iota(jnp.int32, (lanes, lanes), 0) == lax.broadcasted_iota(
        jnp.int32, (lanes, lanes), 1
    )
    tn = (((0,), (0,)), ((), ()))
    weights_all[row_ds(own_at, rows), :] = lax.dot_general(
        dense.astype(BF16), same.astype(F32).astype(BF16), tn, preferred_element_type=F32
    )

    loads[3].wait()
    for load in loads[6:]:
        load.start()

    pl.semaphore_wait(barrier, len(partners))

    def project(k, carry):
        proj_part[k] = jnp.dot(
            attended[...], out_proj[:, cols(k)], preferred_element_type=F32
        ).astype(BF16)
        for s in range(1, tp_count):
            proj_send(k, s).start()
        return carry

    lax.fori_loop(0, chunks, project, 0)

    loads[4].wait()
    loads[5].wait()

    def g_z_send(k, step):
        z_to = z_at(step)
        block = rows_all.at[k, row_ds(own_at, rows), :]
        return remote(block, block, gzs_sem.at[k, z_to], gzr_sem.at[k, z_me], z_dev(z_to))

    def g_z_recv(k, step):
        z_from = z_at(step)
        block = rows_all.at[k, row_ds(line_at + z_from * rows, rows), :]
        return remote(block, block, gzs_sem.at[k, z_from], gzr_sem.at[k, z_from], z_dev(z_from))

    def g_y_send(k, step):
        y_to = y_at(step)
        block = rows_all.at[k, row_ds(line_at, line_rows), :]
        return remote(block, block, gys_sem.at[k, y_to], gyr_sem.at[k, y_me], y_dev(y_to))

    def g_y_recv(k, step):
        y_from = y_at(step)
        block = rows_all.at[k, row_ds(half_at + y_from * line_rows, line_rows), :]
        return remote(block, block, gys_sem.at[k, y_from], gyr_sem.at[k, y_from], y_dev(y_from))

    def g_c_send(k):
        block = rows_all.at[k, row_ds(half_at, half_rows), :]
        return remote(block, block, gcs_sem.at[k], gcr_sem.at[k], core_dev)

    def g_c_recv(k):
        block = rows_all.at[k, row_ds(c_other * half_rows, half_rows), :]
        return remote(block, block, gcs_sem.at[k], gcr_sem.at[k], core_dev)

    gate_acc[...] = jnp.zeros_like(gate_acc)
    up_acc[...] = jnp.zeros_like(up_acc)
    power[...] = jnp.zeros_like(power)

    def first(i, carry):
        @pl.when(i < chunks)
        def _():
            for s in range(1, tp_count):
                proj_recv(i, s).wait_recv()
            total = proj_part[i, row_ds(z_me * rows, rows), :].astype(F32)
            for s in range(1, tp_count):
                total = total + proj_in[i, z_at(s)].astype(F32)
            h = (residual[:, cols(i)].astype(F32) + total).astype(BF16)
            hidden[:, cols(i)] = h
            wide = h.astype(F32)
            rows_all[i, row_ds(own_at, rows), :] = (wide * gain[:, cols(i)]).astype(BF16)
            for s in range(1, tp_count):
                g_z_send(i, s).start()
            power[...] += jnp.sum(wide * wide, axis=1, keepdims=True)

        @pl.when(i == chunks)
        def _():
            factor = lax.rsqrt(power[...] / dim + 1e-05)
            own = weights_all[row_ds(own_at, rows), :]
            at = lax.broadcasted_iota(jnp.int32, own.shape, 1)
            weights_all[row_ds(own_at, rows), :] = jnp.where(at == pool_count, factor, own)
            for s in range(1, tp_count):
                w_z_send(s).start()

        @pl.when((i >= lag) & (i < chunks + lag))
        def _():
            k = i - lag
            for s in range(1, tp_count):
                g_z_recv(k, s).wait_recv()
            for s in range(1, y_count):
                g_y_send(k, s).start()

        @pl.when(i == chunks + lag)
        def _():
            for s in range(1, tp_count):
                w_z_recv(s).wait_recv()
            for s in range(1, y_count):
                w_y_send(s).start()

        @pl.when((i >= 2 * lag) & (i < chunks + 2 * lag))
        def _():
            k = i - 2 * lag
            for s in range(1, y_count):
                g_y_recv(k, s).wait_recv()
            g_c_send(k).start()

        @pl.when(i == chunks + 2 * lag)
        def _():
            for s in range(1, y_count):
                w_y_recv(s).wait_recv()
            w_c_send().start()

        @pl.when(i == 3 * lag)
        def _():
            loads[6].wait()
            loads[7].wait()

        @pl.when(i >= 3 * lag)
        def _():
            k = i - 3 * lag
            g_c_recv(k).wait_recv()
            block = rows_all[k]
            gate_acc[...] += lax.dot_general(
                block, w_gate[0, :, cols(k)], nt, preferred_element_type=F32
            )
            up_acc[...] += lax.dot_general(
                block, w_up[0, :, cols(k)], nt, preferred_element_type=F32
            )

        return carry

    lax.fori_loop(0, chunks + 3 * lag, first, 0)
    w_c_recv().wait_recv()

    def column(at):
        lane = lax.broadcasted_iota(jnp.int32, weights_all.shape, 1)
        return jnp.sum(jnp.where(lane == at, weights_all[...], 0.0), axis=1, keepdims=True)

    factor_all = column(pool_count)
    combine = column(pool_me)
    gate = gate_acc[...] * factor_all
    act[...] = (gate / (1.0 + jnp.exp(-gate)) * (up_acc[...] * factor_all)).astype(BF16)

    def s_c_send(k):
        return remote(
            part_all.at[k, row_ds(c_other * half_rows, half_rows), :],
            core_in.at[k],
            scs_sem.at[k],
            scr_sem.at[k],
            core_dev,
        )

    def s_y_send(k, step):
        y_to = y_at(step)
        return remote(
            core_in.at[k, row_ds(y_to * line_rows, line_rows), :],
            pair_in.at[k, y_me],
            sys_sem.at[k, y_to],
            syr_sem.at[k, y_me],
            y_dev(y_to),
        )

    def s_y_recv(k, step):
        y_from = y_at(step)
        return remote(
            core_in.at[k, row_ds(y_from * line_rows, line_rows), :],
            pair_in.at[k, y_from],
            sys_sem.at[k, y_from],
            syr_sem.at[k, y_from],
            y_dev(y_from),
        )

    def s_z_send(k, step):
        z_to = z_at(step)
        return remote(
            pair_sum.at[k, row_ds(z_to * rows, rows), :],
            line_in.at[k, z_me],
            szs_sem.at[k, z_to],
            szr_sem.at[k, z_me],
            z_dev(z_to),
        )

    def s_z_recv(k, step):
        z_from = z_at(step)
        return remote(
            pair_sum.at[k, row_ds(z_from * rows, rows), :],
            line_in.at[k, z_from],
            szs_sem.at[k, z_from],
            szr_sem.at[k, z_from],
            z_dev(z_from),
        )

    loads[8].wait()

    def second(i, carry):
        @pl.when(i < chunks)
        def _():
            part = jnp.dot(act[...], w_down[0, :, cols(i)], preferred_element_type=F32)
            part_all[i] = (part * combine).astype(BF16)
            s_c_send(i).start()

        @pl.when((i >= lag) & (i < chunks + lag))
        def _():
            k = i - lag
            s_c_send(k).wait_recv()
            core_in[k] = (
                core_in[k].astype(F32)
                + part_all[k, row_ds(half_at, half_rows), :].astype(F32)
            ).astype(BF16)
            for s in range(1, y_count):
                s_y_send(k, s).start()

        @pl.when((i >= 2 * lag) & (i < chunks + 2 * lag))
        def _():
            k = i - 2 * lag
            total = core_in[k, row_ds(y_me * line_rows, line_rows), :].astype(F32)
            for s in range(1, y_count):
                s_y_recv(k, s).wait_recv()
                total = total + pair_in[k, y_at(s)].astype(F32)
            pair_sum[k] = total.astype(BF16)
            for s in range(1, tp_count):
                s_z_send(k, s).start()

        @pl.when(i >= 3 * lag)
        def _():
            k = i - 3 * lag
            total = pair_sum[k, row_ds(z_me * rows, rows), :].astype(F32)
            for s in range(1, tp_count):
                s_z_recv(k, s).wait_recv()
                total = total + line_in[k, z_at(s)].astype(F32)
            out_ref[:, cols(k)] = (hidden[:, cols(k)].astype(F32) + total).astype(BF16)

        return carry

    lax.fori_loop(0, chunks + 3 * lag, second, 0)

    for s in range(1, tp_count):
        w_z_send(s).wait_send()
    for s in range(1, y_count):
        w_y_send(s).wait_send()
    w_c_send().wait_send()

    def drain(k, carry):
        for s in range(1, tp_count):
            proj_send(k, s).wait_send()
            g_z_send(k, s).wait_send()
            s_z_send(k, s).wait_send()
        for s in range(1, y_count):
            g_y_send(k, s).wait_send()
            s_y_send(k, s).wait_send()
        g_c_send(k).wait_send()
        s_c_send(k).wait_send()
        return carry

    lax.fori_loop(0, chunks, drain, 0)


def local(
    pool_count,
    tp_count,
    residual,
    queries,
    new_kv,
    cache,
    cache_len,
    draft_count,
    out_proj,
    norm_gain,
    routes,
    slots,
    route_weights,
    w_gate,
    w_up,
    w_down,
):
    rows, dim = residual.shape
    y_count = pool_count // CORES
    line_rows = tp_count * rows
    half_rows = y_count * line_rows
    all_rows = CORES * half_rows
    hidden_units = w_down.shape[1]
    weight_lanes = pl.cdiv(pool_count + 1, LANES) * LANES
    chunks, lag = 8, 3
    width = dim // chunks
    gain = norm_gain.reshape(1, dim)
    w_gate, w_up = jnp.swapaxes(w_gate, 1, 2), jnp.swapaxes(w_up, 1, 2)
    routes, slots, route_weights = routes.T, slots.T, route_weights.T
    dma = pltpu.SemaphoreType.DMA
    loaded = (residual, queries, new_kv, cache, out_proj, gain, w_gate, w_up, w_down)
    smem = pl.BlockSpec(memory_space=pltpu.SMEM)
    vmem = pl.BlockSpec(memory_space=pltpu.VMEM)
    return pl.pallas_call(
        functools.partial(kernel, pool_count, tp_count, chunks, lag),
        out_shape=jax.ShapeDtypeStruct((rows, dim), BF16),
        in_specs=[smem] * 2 + [vmem] * 3 + [pl.BlockSpec(memory_space=pl.ANY)] * len(loaded),
        out_specs=vmem,
        scratch_shapes=[pltpu.VMEM(a.shape, a.dtype) for a in loaded]
        + [
            pltpu.VMEM((queries.shape[0], queries.shape[1]), BF16),
            pltpu.VMEM((chunks, line_rows, width), BF16),
            pltpu.VMEM((chunks, tp_count, rows, width), BF16),
            pltpu.VMEM((rows, dim), BF16),
            pltpu.VMEM((chunks, all_rows, width), BF16),
            pltpu.VMEM((all_rows, weight_lanes), F32),
            pltpu.VMEM((rows, weight_lanes), F32),
            pltpu.VMEM((all_rows, hidden_units), F32),
            pltpu.VMEM((all_rows, hidden_units), F32),
            pltpu.VMEM((all_rows, hidden_units), BF16),
            pltpu.VMEM((chunks, all_rows, width), BF16),
            pltpu.VMEM((chunks, half_rows, width), BF16),
            pltpu.VMEM((chunks, y_count, line_rows, width), BF16),
            pltpu.VMEM((chunks, line_rows, width), BF16),
            pltpu.VMEM((chunks, tp_count, rows, width), BF16),
            dma((len(loaded),)),
            dma((chunks, tp_count)),
            dma((chunks, tp_count)),
            dma((tp_count,)),
            dma((tp_count,)),
            dma((y_count,)),
            dma((y_count,)),
            dma((2,)),
            dma((chunks, tp_count)),
            dma((chunks, tp_count)),
            dma((chunks, y_count)),
            dma((chunks, y_count)),
            dma((chunks,)),
            dma((chunks,)),
            dma((chunks, tp_count)),
            dma((chunks, tp_count)),
            dma((chunks, y_count)),
            dma((chunks, y_count)),
            dma((chunks,)),
            dma((chunks,)),
        ],
        compiler_params=pltpu.CompilerParams(
            collective_id=0, has_side_effects=True, vmem_limit_bytes=60 * 1024 * 1024
        ),
    )(cache_len, draft_count, routes, slots, route_weights, *loaded)


def solution(mesh):
    in_specs = (
        P(("parts", "pool", "tp"), None),
        P(("parts", "pool"), "tp"),
        P(None, ("parts", "pool"), "tp"),
        P(None, ("parts", "pool"), None, "tp"),
        P(("parts", "pool")),
        P(("parts", "pool")),
        P("tp", None),
        P(),
        P(("parts", "pool", "tp"), None),
        P(("parts", "pool", "tp"), None),
        P(("parts", "pool", "tp"), None),
        P("pool", None, "tp"),
        P("pool", None, "tp"),
        P("pool", "tp", None),
    )
    out_specs = P(("parts", "pool", "tp"), None)
    body = functools.partial(local, mesh.shape["pool"], mesh.shape["tp"])
    return jax.shard_map(body, mesh=mesh, in_specs=in_specs, out_specs=out_specs, check_vma=False)
```
